32 devices in a mesh: seq: 4 (over x, core), exp: 8 (over z, y).
Axes of the slice: x: 2, y: 2, z: 4, core: 2. Of those that a mesh axis runs over, the one named last changes fastest.
Arguments:
- queries: bfloat16 [8, 512, 2048], P('exp', 'seq'), may hold values from -14 to 14
- keys: bfloat16 [8, 512, 2048], P('exp', 'seq'), may hold values from -6 to 6
- values: bfloat16 [8, 512, 2048], P('exp', 'seq'), may hold values from -6 to 6
- out_grad: bfloat16 [8, 512, 2048], P('exp', 'seq'), may hold values from -6 to 6
- norm_gain: float32 [2048], replicated, may hold values from 0.5 to 1.5
- gate_values: float32 [8, 512, 2], P('exp', 'seq'), may hold values from 0.2 to 1
- expert_ids: int32 [8, 512, 2], P('exp', 'seq'), may hold values from 0 to 15, all different within a row; in each aligned block of 128 rows (0 to 127, 128 to 255, ..., all dimensions but the last counted through in order) at most 20 rows name the same one
- tile_offsets: int32 [8, 8, 3], P('exp', 'seq'), may hold values from -2 to 2, as said below
- gate_weight: bfloat16 [8, 4, 2048, 1024], P('exp', 'seq'), may hold values from -0.125 to 0.125
- up_weight: bfloat16 [8, 4, 2048, 1024], P('exp', 'seq'), may hold values from -0.125 to 0.125
- down_weight: bfloat16 [8, 4, 1024, 2048], P('exp', 'seq'), may hold values from -0.125 to 0.125
Outputs:
- key_grad: bfloat16 [8, 512, 2048], P('exp', 'seq')
- value_grad: bfloat16 [8, 512, 2048], P('exp', 'seq')
The draws below stay inside these ranges and needn't reach their ends.
Inputs may be any that keep to these rules, and one draw needn't show every extreme that they name: `expert_ids`: a token's two ids differ; the tokens of one index pair (one device) name one expert at most 20 times. `tile_offsets`: each row holds 3 different offsets, the first of them 0.
All inputs are finite; a program needn't handle non-finite values.
Results may differ from the reference program's by a relative error of at most 0.013.
Values may be sent and summed in bfloat16 or wider, within the bound.
A program may use at most 128 MiB of HBM per device.

```python
import math
import jax
import jax.numpy as jnp
import numpy as np
from jax import lax

HEADS = 16
HEAD_DIM = 128
FF = 2048
TILE = 64
NBR = 3
TOK_DEV = 128
D = 2048
SAMPLES = 8
SEQLEN = 512
NTILES = 8
EXPERTS = 16
FF_PART = 1024
CAP = 20
N_SEQ = 4
N_EXP = 8


def paired_fields(key):
    shape = (SAMPLES, SEQLEN, D)
    key_base = jnp.clip(jax.random.normal(jax.random.fold_in(key, 11), shape, jnp.float32), -6.0, 6.0)
    query_base = jnp.clip(jax.random.normal(jax.random.fold_in(key, 12), shape, jnp.float32), -6.0, 6.0)
    return (key_base, query_base)


def draw_queries(key, part):
    return paired_fields(key)[1].astype(jnp.bfloat16)


def draw_keys(key, part):
    return paired_fields(key)[0].astype(jnp.bfloat16)


def draw_tile_offsets(key, part):
    scores = jax.random.randint(jax.random.fold_in(key, 21), (SAMPLES, NTILES, 4), 0, 1 << 20) * 4
    scores = scores + jnp.arange(4, dtype=jnp.int32)
    ranking = jnp.argsort(scores, axis=-1)
    candidates = jnp.array([-2, -1, 1, 2], jnp.int32)
    picked = candidates[ranking[..., :NBR - 1]]
    return jnp.concatenate([jnp.zeros((SAMPLES, NTILES, 1), jnp.int32), picked], axis=-1)


def steps_of(own_key, dims, shards, low, largest):
    gain = 1.0
    for dim, shards_of in shards:
        heights = jax.random.uniform(jax.random.fold_in(jax.random.fold_in(own_key, 6), dim), (shards_of,), jnp.float32, low / len(shards), largest / len(shards))
        gain = gain * jnp.repeat(jnp.exp(heights), dims[dim] // shards_of).reshape((-1,) + (1,) * (len(dims) - 1 - dim))
    return gain


def deal_out(key, own, number, rows, number_of, top, bound, slope):
    sequence = jax.random.permutation(key, number_of)
    crowded, usual = load_shares(number_of, rows * top, bound, slope, True), load_shares(number_of, rows * top, bound, slope, False)
    places = jnp.arange(number_of)

    def named(tallies, turn):
        used = int((tallies > 0).sum())
        fixed = max(1, used // 4)
        moved = fixed + (places - fixed + turn * (used - fixed)) % max(1, number_of - fixed)
        return jnp.zeros((number_of,), jnp.int32).at[sequence[jnp.where(places < fixed, places, moved)]].set(jnp.asarray(tallies, jnp.int32))

    tallies = jnp.where(number % 4 == 0, named(crowded, number // 4), named(usual, number - number // 4 - 1))
    mixed = jax.random.permutation(jax.random.fold_in(own, 3), number_of)
    donor, receiver = mixed[0:number_of // 2 * 2:2], mixed[1:number_of // 2 * 2:2]
    room = jnp.minimum(tallies[donor] - 1, bound - tallies[receiver]) // 2
    room = jnp.where((donor == sequence[0]) | (receiver == sequence[0]) | (tallies[receiver] == 0), 0, jnp.maximum(room, 0))
    moved = jax.random.randint(jax.random.fold_in(own, 4), (number_of // 2,), 0, 1 << 20) % (room + 1)
    tallies = tallies.at[donor].add(-moved).at[receiver].add(moved)
    labels = jnp.searchsorted(jnp.cumsum(tallies), jnp.arange(rows * top), side="right").astype(jnp.int32)
    grid = labels.reshape(top, rows).T
    grid = grid[jax.random.permutation(jax.random.fold_in(own, 1), rows)]
    turn = jax.random.randint(jax.random.fold_in(own, 2), (rows, 1), 0, top)
    return jnp.take_along_axis(grid, (jnp.arange(top)[None, :] + turn) % top, axis=1)


def load_shares(count, total, limit, lean, full):
    loads = [(1 << 20) // math.isqrt(rank ** lean) + 1 for rank in range(1, count + 1)]
    largest = limit if full else min(limit, max(-(-total // count), total * loads[0] // sum(loads)))
    least = 1 if total - largest >= count - 1 else 0
    counts, spare = [largest] + [least] * (count - 1), total - largest - least * (count - 1)
    while spare > 0:
        movable = [i for i in range(1, count) if counts[i] < largest] or [i for i in range(1, count) if counts[i] < limit]
        pool, remaining = sum([loads[i] for i in movable]), spare
        for i in movable:
            addition = min(limit - counts[i], max(1, remaining * loads[i] // pool), spare)
            counts[i] = counts[i] + addition
            spare = spare - addition
    return np.array(counts)


def scatter_about(rng, dims, scale, most, cuts=(), kind=jnp.bfloat16):
    factor_of = steps_of(rng, dims, cuts, -0.22, 0.18) if cuts else 1.0
    result = jax.random.normal(rng, dims, jnp.float32) * scale * factor_of
    return jnp.minimum(jnp.maximum(result, -most), most).astype(kind)


def setup_inputs(seed: int = 0) -> dict:
    splits = jax.random.split(jax.random.key(seed), 12)
    queries = draw_queries(jax.random.fold_in(splits[11], 71), 0)
    keys = draw_keys(jax.random.fold_in(splits[11], 71), 0)
    values = scatter_about(splits[2], (SAMPLES, SEQLEN, D), 1.0, 6.0, ((0, 8), (1, 4)))
    out_grad = scatter_about(splits[3], (SAMPLES, SEQLEN, D), 1.0, 6.0, ((0, 8), (1, 4)))
    norm_gain = jnp.clip(1.0 + 0.1 * jax.random.normal(splits[4], (D,), jnp.float32), 0.5, 1.5)
    gate_values = jnp.clip(jnp.exp(math.log(1.0) - 1.609438 * jax.random.uniform(splits[5], (SAMPLES, SEQLEN, 2), jnp.float32) ** steps_of(splits[5], (SAMPLES, SEQLEN, 2), ((0, 8), (1, 4)), -0.2, 0.2)), 0.2, 1.0)
    expert_ids_keys = jax.random.split(jax.random.fold_in(splits[6], 1), SAMPLES * SEQLEN // TOK_DEV)
    expert_ids_turns = jax.random.permutation(jax.random.fold_in(splits[6], 3), SAMPLES * SEQLEN // TOK_DEV)
    expert_ids = jax.vmap(lambda own, number: deal_out(jax.random.fold_in(splits[6], 2), own, number, TOK_DEV, EXPERTS, 2, CAP, 2))(expert_ids_keys, expert_ids_turns).reshape((SAMPLES, SEQLEN, 2))
    tile_offsets = draw_tile_offsets(jax.random.fold_in(splits[11], 71), 0)
    gate_weight = scatter_about(splits[8], (N_EXP, N_SEQ, D, FF_PART), D ** -0.5, 0.125, ((0, 8), (1, 4)))
    up_weight = scatter_about(splits[9], (N_EXP, N_SEQ, D, FF_PART), D ** -0.5, 0.125, ((0, 8), (1, 4)))
    down_weight = scatter_about(splits[10], (N_EXP, N_SEQ, FF_PART, D), FF ** -0.5, 0.125, ((0, 8), (1, 4)))
    return {"queries": queries, "keys": keys, "values": values, "out_grad": out_grad, "norm_gain": norm_gain, "gate_values": gate_values, "expert_ids": expert_ids, "tile_offsets": tile_offsets, "gate_weight": gate_weight, "up_weight": up_weight, "down_weight": down_weight}


epsilon = 1e-06

def barrier_round(value):
    return lax.optimization_barrier(value.astype(jnp.bfloat16)).astype(jnp.float32)

def window_operands(query_s, key_s, value_s, offsets):
    tile_total = query_s.shape[0] // TILE
    tile_ids = jnp.arange(tile_total, dtype=jnp.int32)[:, None] + offsets.astype(jnp.int32)
    valid = (tile_ids >= 0) & (tile_ids < tile_total)
    clipped = jnp.clip(tile_ids, 0, tile_total - 1).astype(jnp.int32)
    tile_shape = (tile_total, TILE, HEADS, HEAD_DIM)
    window_shape = (tile_total, NBR * TILE, HEADS, HEAD_DIM)
    query_t = query_s.reshape(tile_shape).astype(jnp.float32)
    key_t = key_s.reshape(tile_shape).astype(jnp.float32)[clipped].reshape(window_shape)
    value_t = value_s.reshape(tile_shape).astype(jnp.float32)[clipped].reshape(window_shape)
    key_mask = jnp.repeat(valid, TILE, axis=1)
    return (query_t, key_t, value_t, key_mask, clipped)

def attention_weights(query_t, key_t, key_mask):
    scores = jnp.einsum('tqhd,tkhd->thqk', query_t, key_t) * HEAD_DIM ** (-0.5)
    scores = jnp.where(key_mask[:, None, None, :], scores, -jnp.inf)
    row_max = lax.optimization_barrier(jnp.max(scores, axis=-1, keepdims=True))
    raised = jnp.exp(scores - row_max)
    return raised / lax.optimization_barrier(jnp.sum(raised, axis=-1, keepdims=True))

def forward_sample(operands):
    query_s, key_s, value_s, offsets = operands
    query_t, key_t, value_t, key_mask, clipped = window_operands(query_s, key_s, value_s, offsets)
    weights_b = barrier_round(attention_weights(query_t, key_t, key_mask))
    attn_out = jnp.einsum('thqk,tkhd->tqhd', weights_b, value_t)
    return attn_out.reshape(query_s.shape[0], HEADS * HEAD_DIM)

def backward_sample(operands):
    query_s, key_s, value_s, offsets, grad_s = operands
    query_t, key_t, value_t, key_mask, clipped = window_operands(query_s, key_s, value_s, offsets)
    tile_total = query_t.shape[0]
    weights_f = attention_weights(query_t, key_t, key_mask)
    weights_b = barrier_round(weights_f)
    grad_t = grad_s.astype(jnp.float32).reshape(tile_total, TILE, HEADS, HEAD_DIM)
    prob_grad = jnp.einsum('tqhd,tkhd->thqk', grad_t, value_t)
    inner_sum = lax.optimization_barrier(jnp.sum(weights_f * prob_grad, axis=-1, keepdims=True))
    score_grad = barrier_round(weights_f * (prob_grad - inner_sum))
    key_part = jnp.einsum('thqk,tqhd->tkhd', score_grad, query_t) * HEAD_DIM ** (-0.5)
    value_part = jnp.einsum('thqk,tqhd->tkhd', weights_b, grad_t)
    flat_ids = clipped.reshape(-1)
    part_shape = (tile_total * NBR, TILE, HEADS, HEAD_DIM)
    tile_shape = (tile_total, TILE, HEADS, HEAD_DIM)
    key_sum = jnp.zeros(tile_shape, jnp.float32).at[flat_ids].add(key_part.reshape(part_shape))
    value_sum = jnp.zeros(tile_shape, jnp.float32).at[flat_ids].add(value_part.reshape(part_shape))
    out_shape = (query_s.shape[0], HEADS * HEAD_DIM)
    return (key_sum.reshape(out_shape).astype(jnp.bfloat16), value_sum.reshape(out_shape).astype(jnp.bfloat16))

def expert_part(rows_in, rows_grad, gate_w, up_w, down_w):
    gate_proj = jnp.dot(rows_in, gate_w, preferred_element_type=jnp.float32)
    up_proj = jnp.dot(rows_in, up_w, preferred_element_type=jnp.float32)
    hidden_grad = jnp.dot(rows_grad, down_w.T, preferred_element_type=jnp.float32)
    sig = jax.nn.sigmoid(gate_proj)
    grad_up = (hidden_grad * gate_proj * sig).astype(jnp.bfloat16)
    grad_gate = (hidden_grad * up_proj * sig * (1.0 + gate_proj * (1.0 - sig))).astype(jnp.bfloat16)
    total = jnp.dot(grad_gate, gate_w.T, preferred_element_type=jnp.float32)
    total = total + jnp.dot(grad_up, up_w.T, preferred_element_type=jnp.float32)
    return total

def reference(queries, keys, values, out_grad, norm_gain, gate_values, expert_ids, tile_offsets, gate_weight, up_weight, down_weight):
    width = HEADS * HEAD_DIM
    attn_out = lax.map(forward_sample, (queries, keys, values, tile_offsets))
    inv_rms = lax.rsqrt(lax.optimization_barrier(jnp.mean(attn_out * attn_out, axis=-1, keepdims=True)) + epsilon)
    unit = attn_out * inv_rms
    normed = (unit * norm_gain).astype(jnp.bfloat16)
    tokens_total = SAMPLES * SEQLEN
    group = N_SEQ // 2
    max_rows = N_SEQ * N_EXP * CAP
    flat_experts = expert_ids.reshape(-1).astype(jnp.int32)
    one_hot = (flat_experts[:, None] == jnp.arange(EXPERTS, dtype=jnp.int32)[None, :]).astype(jnp.int32)
    rank_index = lax.optimization_barrier(jnp.sum(jnp.cumsum(one_hot, axis=0) * one_hot, axis=1)) - 1
    slot_index = (flat_experts * max_rows + rank_index).astype(jnp.int32)
    owner = jnp.full((EXPERTS * max_rows,), -1, jnp.int32)
    owner = owner.at[slot_index].set(jnp.arange(tokens_total * 2, dtype=jnp.int32)).reshape(EXPERTS, max_rows)
    normed_flat = normed.reshape(tokens_total, width)
    grad_flat = out_grad.reshape(tokens_total, width)
    gate_all = gate_weight.reshape(EXPERTS, group, width, FF_PART)
    up_all = up_weight.reshape(EXPERTS, group, width, FF_PART)
    down_all = down_weight.reshape(EXPERTS, group, FF_PART, width)

    def expert_rows(operands):
        gate_w, up_w, down_w, owner_row = operands
        live = owner_row >= 0
        token = jnp.where(live, owner_row // 2, 0).astype(jnp.int32)
        rows_in = jnp.where(live[:, None], normed_flat[token], jnp.zeros((), jnp.bfloat16))
        rows_grad = jnp.where(live[:, None], grad_flat[token], jnp.zeros((), jnp.bfloat16))
        total = jnp.zeros((max_rows, width), jnp.float32)
        for part in range(group):
            total = total + barrier_round(expert_part(rows_in, rows_grad, gate_w[part], up_w[part], down_w[part]))
        return total.astype(jnp.bfloat16)
    returned = lax.map(expert_rows, (gate_all, up_all, down_all, owner))
    route_grad = returned.reshape(EXPERTS * max_rows, width)[slot_index]
    route_grad = route_grad.reshape(SAMPLES, SEQLEN, 2, width).astype(jnp.float32)
    normed_grad = lax.optimization_barrier(jnp.sum(gate_values[..., None] * route_grad, axis=2))
    scaled = normed_grad * norm_gain
    attn_grad = out_grad.astype(jnp.float32) + inv_rms * (scaled - unit * lax.optimization_barrier(jnp.mean(scaled * unit, axis=-1, keepdims=True)))
    attn_grad_b = attn_grad.astype(jnp.bfloat16)
    key_grad, value_grad = lax.map(backward_sample, (queries, keys, values, tile_offsets, attn_grad_b))
    return (key_grad, value_grad)
```

```python
import functools

import jax
import jax.numpy as jnp
from jax import lax
from jax.experimental import pallas as pl
from jax.experimental.pallas import tpu as pltpu
from jax.sharding import PartitionSpec as P

HEAD_DIM = 128
TILE = 64
SUB = 16
MESH = pl.DeviceIdType.MESH

epsilon = 1e-06


def dot(a, b, dims=((1,), (0,))):
    return lax.dot_general(a, b, (dims, ((), ())), preferred_element_type=jnp.float32)


def iota(shape, dim):
    return lax.broadcasted_iota(jnp.int32, shape, dim)


class Plan:
    def __init__(self, local_len, width, seq_count, col_count):
        self.local_len, self.width = local_len, width
        self.seq_count, self.col_count = seq_count, col_count
        self.group = seq_count // 2
        self.heads = width // HEAD_DIM
        experts = 2 * col_count
        capacity = max(2, (5 * local_len + 2 * experts - 1) // (2 * experts))
        self.full = capacity // SUB
        left = capacity % SUB
        self.rest = 0 if left == 0 else 4 if left <= 4 else 8 if left <= 8 else 16
        if self.rest == 16:
            self.full, self.rest = self.full + 1, 0
        self.cuts = SUB // self.rest if self.rest else 0
        self.cut = width // self.cuts if self.rest else 0
        self.packed = self.full * width + self.cut
        self.dests = 2 * col_count
        self.rows = self.dests * SUB
        self.pieces = 4


def expert_of(plan, dest):
    return 2 * (dest % plan.col_count) + dest // plan.col_count


def partner(plan, dest, member):
    return (dest // plan.col_count * plan.group + member, dest % plan.col_count)


def place():
    return lax.axis_index("seq"), lax.axis_index("exp")


def crosses(plan, seq, side):
    other = seq + side
    return (other >= 0) & (other < plan.seq_count) & (other // plan.group != seq // plan.group)


def greet(plan):
    seq, exp = place()
    member = seq % plan.group
    mine = seq // plan.group * plan.col_count + exp
    barrier = pltpu.get_barrier_semaphore()

    def step(j, carry):
        dest = (mine + j) % plan.dests
        pl.semaphore_signal(barrier, inc=1, device_id=partner(plan, dest, member), device_id_type=MESH)
        return carry

    lax.fori_loop(1, plan.dests, step, 0)
    for other in range(1, plan.group):
        to = seq // plan.group * plan.group + (member + other) % plan.group
        pl.semaphore_signal(barrier, inc=1, device_id=(to, exp), device_id_type=MESH)
    low, high = crosses(plan, seq, -1), crosses(plan, seq, 1)

    @pl.when(low)
    def _():
        pl.semaphore_signal(barrier, inc=1, device_id=(seq - 1, exp), device_id_type=MESH)

    @pl.when(high)
    def _():
        pl.semaphore_signal(barrier, inc=1, device_id=(seq + 1, exp), device_id_type=MESH)

    peers = plan.dests - 1 + plan.group - 1
    pl.semaphore_wait(barrier, peers + jnp.where(low, 1, 0) + jnp.where(high, 1, 0))


def remote(src, dst, send, recv, to):
    return pltpu.make_async_remote_copy(
        src_ref=src, dst_ref=dst, send_sem=send, recv_sem=recv, device_id=to, device_id_type=MESH
    )


def window_mask(plan, offs_ref, seq):
    tiles = plan.local_len // TILE
    key_tile = iota((3 * plan.local_len, plan.local_len), 0) // TILE
    query_tile = iota((3 * plan.local_len, plan.local_len), 1) // TILE
    mask = jnp.zeros((3 * plan.local_len, plan.local_len), jnp.int32)
    for i in range(tiles):
        for m in range(offs_ref.shape[1]):
            offset = offs_ref[i, m]
            whole = seq * tiles + i + offset
            inside = (whole >= 0) & (whole < tiles * plan.seq_count)
            target = jnp.where(inside, tiles + i + offset, -1)
            mask = mask | ((query_tile == i) & (key_tile == target)).astype(jnp.int32)
    return mask > 0


def forward_kernel(
    plan, offs_ref, ids_ref, q_ref, k_ref, v_ref, grad_ref, gain_ref,
    recv_ref, prob_ref, unit_ref, inv_ref, vx_ref,
    kx_ref, normed_ref, sbuf, out_ref,
    halo_send, halo_recv, send_sem, recv_sem, fsend, frecv,
):
    seq, exp = place()
    local_len, width, rows = plan.local_len, plan.width, plan.rows
    member = seq % plan.group
    mine = seq // plan.group * plan.col_count + exp
    last = plan.seq_count - 1
    greet(plan)

    def halo(right):
        to = (seq + 1, exp) if right else (seq - 1, exp)
        slot = 0 if right else 2
        d = 0 if right else 1
        return [
            remote(ref, ext.at[slot], halo_send.at[i, d], halo_recv.at[i, d], to)
            for i, (ref, ext) in enumerate(((k_ref, kx_ref), (v_ref, vx_ref)))
        ]

    @pl.when(seq < last)
    def _():
        for c in halo(True):
            c.start()

    @pl.when(seq > 0)
    def _():
        for c in halo(False):
            c.start()

    expert = expert_of(plan, iota((plan.dests, local_len), 0))
    routed = ((ids_ref[0:1, :] == expert) | (ids_ref[1:2, :] == expert)).astype(jnp.float32)
    before = (iota((local_len, local_len), 0) < iota((local_len, local_len), 1)).astype(jnp.bfloat16)
    rank = dot(routed.astype(jnp.bfloat16), before)
    held = jnp.where(routed > 0, rank, -1.0).astype(jnp.bfloat16)
    spread = (iota((rows, plan.dests), 0) // SUB == iota((rows, plan.dests), 1)).astype(jnp.bfloat16)
    slot_of = dot(spread, held).astype(jnp.int32)
    row = iota((rows, local_len), 0) % SUB

    def pack(which, rows_ref):
        for f in range(plan.full):
            pick = (slot_of == row + f * SUB).astype(jnp.bfloat16)
            sbuf[which, :, f * width : (f + 1) * width] = dot(pick, rows_ref[...]).astype(jnp.bfloat16)
        if plan.rest:
            total = None
            for c in range(plan.cuts):
                pick = (slot_of == row % plan.rest + plan.full * SUB) & (row // plan.rest == c)
                part = dot(pick.astype(jnp.bfloat16), rows_ref[:, c * plan.cut : (c + 1) * plan.cut])
                total = part if total is None else total + part
            sbuf[which, :, plan.full * width :] = total.astype(jnp.bfloat16)

    def chunk(dest):
        return pl.ds(pl.multiple_of(dest * SUB, SUB), SUB)

    def landed(dest):
        return pl.ds(pl.multiple_of((member * plan.dests + dest) * SUB, SUB), SUB)

    def sending(which, dest):
        return remote(
            sbuf.at[which, chunk(dest)],
            recv_ref.at[which, landed(mine)],
            send_sem.at[which, dest],
            recv_sem.at[which, mine],
            partner(plan, dest, member),
        )

    def arriving(which, source):
        return remote(
            sbuf.at[which, chunk(source)],
            recv_ref.at[which, landed(source)],
            send_sem.at[which, source],
            recv_sem.at[which, source],
            partner(plan, source, member),
        )

    def send_all(which):
        def step(j, carry):
            sending(which, (mine + j) % plan.dests).start()
            return carry

        lax.fori_loop(1, plan.dests, step, 0)
        recv_ref[which, landed(mine), :] = sbuf[which, chunk(mine), :]

    span = plan.dests // plan.pieces

    def passing(which, piece, other, owner):
        at = pl.ds(pl.multiple_of((owner * plan.dests + piece * span) * SUB, SUB), span * SUB)
        to = (seq // plan.group * plan.group + (member + other) % plan.group, exp)
        return remote(
            recv_ref.at[which, at],
            recv_ref.at[which, at],
            fsend.at[which, piece, other],
            frecv.at[which, piece, owner],
            to,
        )

    def pass_on(which):
        for piece in range(plan.pieces):
            def step(j, carry):
                source = piece * span + j

                @pl.when(source != mine)
                def _():
                    arriving(which, source).wait_recv()

                return carry

            lax.fori_loop(0, span, step, 0)
            for other in range(1, plan.group):
                passing(which, piece, other, member).start()

    def finish(which):
        for piece in range(plan.pieces):
            for other in range(1, plan.group):
                owner = (member + plan.group - other) % plan.group
                passing(which, piece, other, owner).wait_recv()
                passing(which, piece, other, member).wait_send()

        def step(j, carry):
            sending(which, (mine + j) % plan.dests).wait_send()
            return carry

        lax.fori_loop(1, plan.dests, step, 0)

    pack(1, grad_ref)
    send_all(1)

    kx_ref[1] = k_ref[...]
    vx_ref[1] = v_ref[...]
    blank = jnp.zeros((local_len, width), jnp.bfloat16)

    @pl.when(seq == 0)
    def _():
        kx_ref[0] = blank
        vx_ref[0] = blank

    @pl.when(seq == last)
    def _():
        kx_ref[2] = blank
        vx_ref[2] = blank

    mask = window_mask(plan, offs_ref, seq)

    @pl.when(seq > 0)
    def _():
        for c in halo(True):
            c.wait_recv()

    @pl.when(seq < last)
    def _():
        for c in halo(False):
            c.wait_recv()

    per = 4

    def heads(i, carry):
        for u in range(per):
            h = i * per + u
            at = pl.ds(pl.multiple_of(h * HEAD_DIM, HEAD_DIM), HEAD_DIM)
            kh = kx_ref[:, :, at].reshape(3 * local_len, HEAD_DIM)
            vh = vx_ref[:, :, at].reshape(3 * local_len, HEAD_DIM)
            scores = dot(kh, q_ref[:, at], ((1,), (1,))) * HEAD_DIM ** (-0.5)
            scores = jnp.where(mask, scores, -jnp.inf)
            raised = jnp.exp(scores - jnp.max(scores, axis=0, keepdims=True))
            weights = raised / jnp.sum(raised, axis=0, keepdims=True)
            prob_ref[h] = weights
            out_ref[:, at] = dot(weights.astype(jnp.bfloat16), vh, ((0,), (0,)))
        return carry

    lax.fori_loop(0, plan.heads // per, heads, 0)

    attn_out = out_ref[...]
    inv_rms = lax.rsqrt(jnp.mean(attn_out * attn_out, axis=-1, keepdims=True) + epsilon)
    unit = attn_out * inv_rms
    unit_ref[...] = unit
    inv_ref[...] = jnp.broadcast_to(inv_rms, (local_len, 128))
    normed_ref[...] = (unit * gain_ref[...]).astype(jnp.bfloat16)
    pack(0, normed_ref)
    send_all(0)
    pass_on(1)
    pass_on(0)

    @pl.when(seq < last)
    def _():
        for c in halo(True):
            c.wait_send()

    @pl.when(seq > 0)
    def _():
        for c in halo(False):
            c.wait_send()

    finish(1)
    finish(0)


def backward_kernel(
    plan, ids_ref, gates_ref, part_ref, q_ref, grad_ref, gain_ref, prob_ref, unit_ref, inv_ref, vx_ref,
    key_ref, value_ref,
    rbuf, ssum, back, ag_ref, mid_ref, side_ref, side_in,
    send_sem, recv_sem, fsend, frecv, side_send, side_recv,
):
    seq, exp = place()
    local_len, width, rows = plan.local_len, plan.width, plan.rows
    member = seq % plan.group
    mine = seq // plan.group * plan.col_count + exp
    last = plan.seq_count - 1
    greet(plan)
    span = plan.dests // plan.pieces * SUB

    def summing(piece, other):
        to_member = (member + other) % plan.group
        return remote(
            part_ref.at[pl.ds(pl.multiple_of(to_member * rows + piece * span, SUB), span)],
            rbuf.at[other, pl.ds(piece * span, span)],
            fsend.at[piece, other],
            frecv.at[piece, other],
            (seq // plan.group * plan.group + to_member, exp),
        )

    for piece in range(plan.pieces):
        for other in range(1, plan.group):
            summing(piece, other).start()

    def chunk(dest):
        return pl.ds(pl.multiple_of(dest * SUB, SUB), SUB)

    def sending(dest):
        return remote(
            ssum.at[chunk(dest)], back.at[chunk(mine)], send_sem.at[dest], recv_sem.at[mine],
            partner(plan, dest, member),
        )

    def arriving(source):
        return remote(
            ssum.at[chunk(source)], back.at[chunk(source)], send_sem.at[source], recv_sem.at[source],
            partner(plan, source, member),
        )

    for piece in range(plan.pieces):
        for other in range(1, plan.group):
            summing(piece, other).wait_recv()
        at = pl.ds(piece * span, span)
        total = part_ref[pl.ds(pl.multiple_of(member * rows + piece * span, SUB), span), :].astype(jnp.float32)
        for other in range(1, plan.group):
            total = total + rbuf[other, at, :].astype(jnp.float32)
        ssum[at, :] = total.astype(jnp.bfloat16)

        def step(j, carry):
            dest = piece * (span // SUB) + j

            @pl.when(dest != mine)
            def _():
                sending(dest).start()

            return carry

        lax.fori_loop(0, span // SUB, step, 0)
    back[chunk(mine), :] = ssum[chunk(mine), :]

    blank = jnp.zeros((2, local_len, width), jnp.bfloat16)

    @pl.when(seq == 0)
    def _():
        side_in[0] = blank

    @pl.when(seq == last)
    def _():
        side_in[1] = blank

    expert = expert_of(plan, iota((local_len, plan.dests), 1))
    named = [ids_ref[:, j : j + 1] == expert for j in range(2)]
    routed = (named[0] | named[1]).astype(jnp.bfloat16)
    before = (iota((local_len, local_len), 1) < iota((local_len, local_len), 0)).astype(jnp.bfloat16)
    rank = dot(before, routed)
    spread = (iota((plan.dests, rows), 1) // SUB == iota((plan.dests, rows), 0)).astype(jnp.bfloat16)
    row = iota((local_len, rows), 1) % SUB
    slots = [
        dot(jnp.where(named[j], rank, -1.0).astype(jnp.bfloat16), spread).astype(jnp.int32) for j in range(2)
    ]

    def wait_back(j, carry):
        arriving((mine + j) % plan.dests).wait_recv()
        return carry

    lax.fori_loop(1, plan.dests, wait_back, 0)

    pieces = []
    blocks = plan.cuts if plan.rest else 1
    step_width = width // blocks
    for c in range(blocks):
        total = None
        for j in range(2):
            got = None
            for f in range(plan.full):
                pick = (slots[j] == row + f * SUB).astype(jnp.bfloat16)
                part = dot(pick, back[:, f * width + c * step_width : f * width + (c + 1) * step_width])
                got = part if got is None else got + part
            if plan.rest:
                pick = (slots[j] == row % plan.rest + plan.full * SUB) & (row // plan.rest == c)
                part = dot(pick.astype(jnp.bfloat16), back[:, plan.full * width :])
                got = part if got is None else got + part
            got = gates_ref[:, j : j + 1] * got
            total = got if total is None else total + got
        pieces.append(total)
    normed_grad = jnp.concatenate(pieces, axis=1)
    scaled = normed_grad * gain_ref[...]
    unit = unit_ref[...]
    inner = jnp.mean(scaled * unit, axis=-1, keepdims=True)
    attn_grad = grad_ref[...].astype(jnp.float32) + inv_ref[:, 0:1] * (scaled - unit * inner)
    ag_ref[...] = attn_grad.astype(jnp.bfloat16)

    parts = 4
    per = plan.heads // parts

    def side_copy(p, right):
        cols = pl.ds(p * per * HEAD_DIM, per * HEAD_DIM)
        d = 1 if right else 0
        to = (seq + 1, exp) if right else (seq - 1, exp)
        return remote(
            side_ref.at[d, :, :, cols], side_in.at[1 - d, :, :, cols],
            side_send.at[d, p], side_recv.at[1 - d, p], to,
        )

    for p in range(parts):
        for u in range(per):
            h = p * per + u
            at = slice(h * HEAD_DIM, (h + 1) * HEAD_DIM)
            vh = vx_ref[:, :, at].reshape(3 * local_len, HEAD_DIM)
            weights = prob_ref[h]
            grad_h = ag_ref[:, at]
            prob_grad = dot(vh, grad_h, ((1,), (1,)))
            inner_sum = jnp.sum(weights * prob_grad, axis=0, keepdims=True)
            score_grad = (weights * (prob_grad - inner_sum)).astype(jnp.bfloat16)
            key_part = dot(score_grad, q_ref[:, at]) * HEAD_DIM ** (-0.5)
            value_part = dot(weights.astype(jnp.bfloat16), grad_h)
            for i, part in enumerate((key_part, value_part)):
                side_ref[0, i, :, at] = part[:local_len].astype(jnp.bfloat16)
                mid_ref[i, :, at] = part[local_len : 2 * local_len]
                side_ref[1, i, :, at] = part[2 * local_len :].astype(jnp.bfloat16)

        @pl.when(seq > 0)
        def _():
            side_copy(p, False).start()

        @pl.when(seq < last)
        def _():
            side_copy(p, True).start()

    for p in range(parts):
        @pl.when(seq > 0)
        def _():
            side_copy(p, True).wait_recv()

        @pl.when(seq < last)
        def _():
            side_copy(p, False).wait_recv()

        at = slice(p * per * HEAD_DIM, (p + 1) * per * HEAD_DIM)
        for i, ref in enumerate((key_ref, value_ref)):
            total = mid_ref[i, :, at] + side_in[0, i, :, at].astype(jnp.float32)
            ref[:, at] = (total + side_in[1, i, :, at].astype(jnp.float32)).astype(jnp.bfloat16)

    for p in range(parts):
        @pl.when(seq > 0)
        def _():
            side_copy(p, False).wait_send()

        @pl.when(seq < last)
        def _():
            side_copy(p, True).wait_send()

    for piece in range(plan.pieces):
        for other in range(1, plan.group):
            summing(piece, other).wait_send()

    def wait_sent(j, carry):
        sending((mine + j) % plan.dests).wait_send()
        return carry

    lax.fori_loop(1, plan.dests, wait_sent, 0)


def expert_part(rows_in, rows_grad, gate_w, up_w, down_w):
    part_width = gate_w.shape[1]
    both_w = jnp.concatenate([gate_w, up_w], axis=1)
    projected = jnp.dot(rows_in, both_w, preferred_element_type=jnp.float32)
    gate_proj = projected[:, :part_width]
    up_proj = projected[:, part_width:]
    hidden_grad = jnp.einsum("rd,fd->rf", rows_grad, down_w, preferred_element_type=jnp.float32)
    sig = jax.nn.sigmoid(gate_proj)
    grad_up = (hidden_grad * gate_proj * sig).astype(jnp.bfloat16)
    grad_gate = (hidden_grad * up_proj * sig * (1.0 + gate_proj * (1.0 - sig))).astype(jnp.bfloat16)
    both_grad = jnp.concatenate([grad_gate, grad_up], axis=1)
    total = jnp.einsum("rf,df->rd", both_grad, both_w, preferred_element_type=jnp.float32)
    return total.astype(jnp.bfloat16)


def unpacked(plan, packed):
    lead = packed.shape[0] // SUB
    blocks = [packed[:, f * plan.width : (f + 1) * plan.width] for f in range(plan.full)]
    if plan.rest:
        rest = packed[:, plan.full * plan.width :].reshape(lead, plan.cuts, plan.rest, plan.cut)
        blocks.append(rest.transpose(0, 2, 1, 3).reshape(lead * plan.rest, plan.width))
    return jnp.concatenate(blocks, axis=0)


def repacked(plan, rows, lead):
    blocks = [rows[f * lead * SUB : (f + 1) * lead * SUB] for f in range(plan.full)]
    if plan.rest:
        rest = rows[plan.full * lead * SUB :].reshape(lead, plan.rest, plan.cuts, plan.cut)
        blocks.append(rest.transpose(0, 2, 1, 3).reshape(lead * SUB, plan.cut))
    return jnp.concatenate(blocks, axis=1)


def on_device(
    queries,
    keys,
    values,
    out_grad,
    norm_gain,
    gate_values,
    expert_ids,
    tile_offsets,
    gate_weight,
    up_weight,
    down_weight,
):
    local_len, width = queries.shape[1:]
    plan = Plan(local_len, width, lax.axis_size("seq"), lax.axis_size("exp"))
    gain = norm_gain.reshape(1, width)
    group, rows, packed = plan.group, plan.rows, plan.packed
    vmem = pl.BlockSpec(memory_space=pltpu.VMEM)
    smem = pl.BlockSpec(memory_space=pltpu.SMEM)
    bf16, f32 = jnp.bfloat16, jnp.float32
    dma = pltpu.SemaphoreType.DMA
    recv, prob, unit, inv, vx = pl.pallas_call(
        functools.partial(forward_kernel, plan),
        out_shape=(
            jax.ShapeDtypeStruct((2, group * rows, packed), bf16),
            jax.ShapeDtypeStruct((plan.heads, 3 * local_len, local_len), f32),
            jax.ShapeDtypeStruct((local_len, width), f32),
            jax.ShapeDtypeStruct((local_len, 128), f32),
            jax.ShapeDtypeStruct((3, local_len, width), bf16),
        ),
        in_specs=[smem] + [vmem] * 6,
        out_specs=(vmem,) * 5,
        scratch_shapes=[
            pltpu.VMEM((3, local_len, width), bf16),
            pltpu.VMEM((local_len, width), bf16),
            pltpu.VMEM((2, rows, packed), bf16),
            pltpu.VMEM((local_len, width), f32),
            dma((2, 2)),
            dma((2, 2)),
            dma((2, plan.dests)),
            dma((2, plan.dests)),
            dma((2, plan.pieces, group)),
            dma((2, plan.pieces, group)),
        ],
        compiler_params=pltpu.CompilerParams(
            collective_id=0, has_side_effects=True, vmem_limit_bytes=56 * 2**20
        ),
        name="attend_and_dispatch",
    )(tile_offsets[0], expert_ids[0].T, queries[0], keys[0], values[0], out_grad[0], gain)
    partial_value = expert_part(
        unpacked(plan, recv[0]), unpacked(plan, recv[1]), gate_weight[0, 0], up_weight[0, 0], down_weight[0, 0]
    )
    partial_value = repacked(plan, partial_value, group * plan.dests)
    key_out, value_out = pl.pallas_call(
        functools.partial(backward_kernel, plan),
        out_shape=(jax.ShapeDtypeStruct((local_len, width), bf16),) * 2,
        in_specs=[vmem] * 10,
        out_specs=(vmem,) * 2,
        scratch_shapes=[
            pltpu.VMEM((group, rows, packed), bf16),
            pltpu.VMEM((rows, packed), bf16),
            pltpu.VMEM((rows, packed), bf16),
            pltpu.VMEM((local_len, width), bf16),
            pltpu.VMEM((2, local_len, width), f32),
            pltpu.VMEM((2, 2, local_len, width), bf16),
            pltpu.VMEM((2, 2, local_len, width), bf16),
            dma((plan.dests,)),
            dma((plan.dests,)),
            dma((plan.pieces, group)),
            dma((plan.pieces, group)),
            dma((2, 4)),
            dma((2, 4)),
        ],
        compiler_params=pltpu.CompilerParams(
            collective_id=1, has_side_effects=True, vmem_limit_bytes=56 * 2**20
        ),
        name="combine_and_attend_back",
    )(expert_ids[0], gate_values[0], partial_value, queries[0], out_grad[0], gain, prob, unit, inv, vx)
    return (key_out[None], value_out[None])


def solution(mesh):
    return jax.shard_map(
        on_device,
        mesh=mesh,
        in_specs=(
            P("exp", "seq", None),
            P("exp", "seq", None),
            P("exp", "seq", None),
            P("exp", "seq", None),
            P(),
            P("exp", "seq", None),
            P("exp", "seq", None),
            P("exp", "seq", None),
            P("exp", "seq", None, None),
            P("exp", "seq", None, None),
            P("exp", "seq", None, None),
        ),
        out_specs=(P("exp", "seq", None), P("exp", "seq", None)),
        check_vma=False,
    )
```

```python
import functools

import jax
import jax.numpy as jnp
from jax import lax
from jax.experimental import pallas as pl
from jax.experimental.pallas import tpu as pltpu
from jax.sharding import PartitionSpec as P

HEAD_DIM = 128
TILE = 64
SUB = 16
MESH = pl.DeviceIdType.MESH

epsilon = 1e-06


def dot(a, b, dims=((1,), (0,))):
    return lax.dot_general(a, b, (dims, ((), ())), preferred_element_type=jnp.float32)


def iota(shape, dim):
    return lax.broadcasted_iota(jnp.int32, shape, dim)


class Plan:
    def __init__(self, local_len, width, seq_count, col_count):
        self.local_len, self.width = local_len, width
        self.seq_count, self.col_count = seq_count, col_count
        self.group = seq_count // 2
        self.heads = width // HEAD_DIM
        experts = 2 * col_count
        capacity = max(2, (5 * local_len + 2 * experts - 1) // (2 * experts))
        self.full = capacity // SUB
        left = capacity % SUB
        self.rest = 0 if left == 0 else 4 if left <= 4 else 8 if left <= 8 else 16
        if self.rest == 16:
            self.full, self.rest = self.full + 1, 0
        self.cuts = SUB // self.rest if self.rest else 0
        self.cut = width // self.cuts if self.rest else 0
        self.packed = self.full * width + self.cut
        self.dests = 2 * col_count
        self.rows = self.dests * SUB
        self.pieces = 4
        self.lead = min(32, self.group * self.dests)
        self.blocks = self.group * self.dests // self.lead
        self.block_rows = self.lead * (self.full * SUB + self.rest)


def expert_of(plan, dest):
    return 2 * (dest % plan.col_count) + dest // plan.col_count


def partner(plan, dest, member):
    return (dest // plan.col_count * plan.group + member, dest % plan.col_count)


def place():
    return lax.axis_index("seq"), lax.axis_index("exp")


def crosses(plan, seq, side):
    other = seq + side
    return (other >= 0) & (other < plan.seq_count) & (other // plan.group != seq // plan.group)


def greet(plan):
    seq, exp = place()
    member = seq % plan.group
    mine = seq // plan.group * plan.col_count + exp
    barrier = pltpu.get_barrier_semaphore()

    def step(j, carry):
        dest = (mine + j) % plan.dests
        pl.semaphore_signal(barrier, inc=1, device_id=partner(plan, dest, member), device_id_type=MESH)
        return carry

    lax.fori_loop(1, plan.dests, step, 0)
    for other in range(1, plan.group):
        to = seq // plan.group * plan.group + (member + other) % plan.group
        pl.semaphore_signal(barrier, inc=1, device_id=(to, exp), device_id_type=MESH)
    low, high = crosses(plan, seq, -1), crosses(plan, seq, 1)

    @pl.when(low)
    def _():
        pl.semaphore_signal(barrier, inc=1, device_id=(seq - 1, exp), device_id_type=MESH)

    @pl.when(high)
    def _():
        pl.semaphore_signal(barrier, inc=1, device_id=(seq + 1, exp), device_id_type=MESH)

    peers = plan.dests - 1 + plan.group - 1
    pl.semaphore_wait(barrier, peers + jnp.where(low, 1, 0) + jnp.where(high, 1, 0))


def remote(src, dst, send, recv, to):
    return pltpu.make_async_remote_copy(
        src_ref=src, dst_ref=dst, send_sem=send, recv_sem=recv, device_id=to, device_id_type=MESH
    )


def window_mask(plan, offs_ref, seq):
    tiles = plan.local_len // TILE
    key_tile = iota((3 * plan.local_len, plan.local_len), 0) // TILE
    query_tile = iota((3 * plan.local_len, plan.local_len), 1) // TILE
    mask = jnp.zeros((3 * plan.local_len, plan.local_len), jnp.int32)
    for i in range(tiles):
        for m in range(offs_ref.shape[1]):
            offset = offs_ref[i, m]
            whole = seq * tiles + i + offset
            inside = (whole >= 0) & (whole < tiles * plan.seq_count)
            target = jnp.where(inside, tiles + i + offset, -1)
            mask = mask | ((query_tile == i) & (key_tile == target)).astype(jnp.int32)
    return mask > 0


def forward_kernel(
    plan, offs_ref, ids_ref, q_ref, k_ref, v_ref, grad_ref, gain_ref, gate_hbm, up_hbm, down_hbm,
    part_ref, prob_ref, unit_ref, inv_ref, vx_ref,
    recv_ref, kx_ref, normed_ref, sbuf, out_ref,
    gate_ref, up_ref, down_ref, rows_ref, hidden_ref, both_ref, weight_sem,
    halo_send, halo_recv, send_sem, recv_sem, fsend, frecv,
):
    seq, exp = place()
    local_len, width, rows = plan.local_len, plan.width, plan.rows
    member = seq % plan.group
    mine = seq // plan.group * plan.col_count + exp
    last = plan.seq_count - 1
    weights = [
        pltpu.make_async_copy(src, dst, weight_sem.at[i])
        for i, (src, dst) in enumerate(((down_hbm, down_ref), (gate_hbm, gate_ref), (up_hbm, up_ref)))
    ]
    for c in weights:
        c.start()
    greet(plan)

    def halo(right):
        to = (seq + 1, exp) if right else (seq - 1, exp)
        slot = 0 if right else 2
        d = 0 if right else 1
        return [
            remote(ref, ext.at[slot], halo_send.at[i, d], halo_recv.at[i, d], to)
            for i, (ref, ext) in enumerate(((k_ref, kx_ref), (v_ref, vx_ref)))
        ]

    @pl.when(seq < last)
    def _():
        for c in halo(True):
            c.start()

    @pl.when(seq > 0)
    def _():
        for c in halo(False):
            c.start()

    expert = expert_of(plan, iota((plan.dests, local_len), 0))
    routed = ((ids_ref[0:1, :] == expert) | (ids_ref[1:2, :] == expert)).astype(jnp.float32)
    before = (iota((local_len, local_len), 0) < iota((local_len, local_len), 1)).astype(jnp.bfloat16)
    rank = dot(routed.astype(jnp.bfloat16), before)
    held = jnp.where(routed > 0, rank, -1.0).astype(jnp.bfloat16)
    spread = (iota((rows, plan.dests), 0) // SUB == iota((rows, plan.dests), 1)).astype(jnp.bfloat16)
    slot_of = dot(spread, held).astype(jnp.int32)
    row = iota((rows, local_len), 0) % SUB

    def pack(which, rows_ref):
        for f in range(plan.full):
            pick = (slot_of == row + f * SUB).astype(jnp.bfloat16)
            sbuf[which, :, f * width : (f + 1) * width] = dot(pick, rows_ref[...]).astype(jnp.bfloat16)
        if plan.rest:
            total = None
            for c in range(plan.cuts):
                pick = (slot_of == row % plan.rest + plan.full * SUB) & (row // plan.rest == c)
                part = dot(pick.astype(jnp.bfloat16), rows_ref[:, c * plan.cut : (c + 1) * plan.cut])
                total = part if total is None else total + part
            sbuf[which, :, plan.full * width :] = total.astype(jnp.bfloat16)

    def chunk(dest):
        return pl.ds(pl.multiple_of(dest * SUB, SUB), SUB)

    def landed(dest):
        return pl.ds(pl.multiple_of((member * plan.dests + dest) * SUB, SUB), SUB)

    def sending(which, dest):
        return remote(
            sbuf.at[which, chunk(dest)],
            recv_ref.at[which, landed(mine)],
            send_sem.at[which, dest],
            recv_sem.at[which, mine],
            partner(plan, dest, member),
        )

    def arriving(which, source):
        return remote(
            sbuf.at[which, chunk(source)],
            recv_ref.at[which, landed(source)],
            send_sem.at[which, source],
            recv_sem.at[which, source],
            partner(plan, source, member),
        )

    def send_all(which):
        def step(j, carry):
            sending(which, (mine + j) % plan.dests).start()
            return carry

        lax.fori_loop(1, plan.dests, step, 0)
        recv_ref[which, landed(mine), :] = sbuf[which, chunk(mine), :]

    span = plan.dests // plan.pieces

    def passing(which, piece, other, owner):
        at = pl.ds(pl.multiple_of((owner * plan.dests + piece * span) * SUB, SUB), span * SUB)
        to = (seq // plan.group * plan.group + (member + other) % plan.group, exp)
        return remote(
            recv_ref.at[which, at],
            recv_ref.at[which, at],
            fsend.at[which, piece, other],
            frecv.at[which, piece, owner],
            to,
        )

    def pass_on(which):
        for piece in range(plan.pieces):
            def step(j, carry):
                source = piece * span + j

                @pl.when(source != mine)
                def _():
                    arriving(which, source).wait_recv()

                return carry

            lax.fori_loop(0, span, step, 0)
            for other in range(1, plan.group):
                passing(which, piece, other, member).start()

    def forwarded(which):
        for piece in range(plan.pieces):
            for other in range(1, plan.group):
                owner = (member + plan.group - other) % plan.group
                passing(which, piece, other, owner).wait_recv()

    def finish(which):
        for piece in range(plan.pieces):
            for other in range(1, plan.group):
                passing(which, piece, other, member).wait_send()

        def step(j, carry):
            sending(which, (mine + j) % plan.dests).wait_send()
            return carry

        lax.fori_loop(1, plan.dests, step, 0)

    pack(1, grad_ref)
    send_all(1)

    kx_ref[1] = k_ref[...]
    vx_ref[1] = v_ref[...]
    blank = jnp.zeros((local_len, width), jnp.bfloat16)

    @pl.when(seq == 0)
    def _():
        kx_ref[0] = blank
        vx_ref[0] = blank

    @pl.when(seq == last)
    def _():
        kx_ref[2] = blank
        vx_ref[2] = blank

    mask = window_mask(plan, offs_ref, seq)

    @pl.when(seq > 0)
    def _():
        for c in halo(True):
            c.wait_recv()

    @pl.when(seq < last)
    def _():
        for c in halo(False):
            c.wait_recv()

    per = 4

    def heads(i, carry):
        for u in range(per):
            h = i * per + u
            at = pl.ds(pl.multiple_of(h * HEAD_DIM, HEAD_DIM), HEAD_DIM)
            kh = kx_ref[:, :, at].reshape(3 * local_len, HEAD_DIM)
            vh = vx_ref[:, :, at].reshape(3 * local_len, HEAD_DIM)
            scores = dot(kh, q_ref[:, at], ((1,), (1,))) * HEAD_DIM ** (-0.5)
            scores = jnp.where(mask, scores, -jnp.inf)
            raised = jnp.exp(scores - jnp.max(scores, axis=0, keepdims=True))
            weights = raised / jnp.sum(raised, axis=0, keepdims=True)
            prob_ref[h] = weights
            out_ref[:, at] = dot(weights.astype(jnp.bfloat16), vh, ((0,), (0,)))
        return carry

    lax.fori_loop(0, plan.heads // per, heads, 0)

    attn_out = out_ref[...]
    inv_rms = lax.rsqrt(jnp.mean(attn_out * attn_out, axis=-1, keepdims=True) + epsilon)
    unit = attn_out * inv_rms
    unit_ref[...] = unit
    inv_ref[...] = jnp.broadcast_to(inv_rms, (local_len, 128))
    normed_ref[...] = (unit * gain_ref[...]).astype(jnp.bfloat16)
    pack(0, normed_ref)
    send_all(0)
    lead, full_rows = plan.lead, plan.lead * plan.full * SUB
    rest_rows, block = plan.lead * plan.rest, plan.block_rows
    hidden_width = gate_ref.shape[1]

    def rest_pick(cut, shape, out_dim):
        out, into = iota(shape, out_dim), iota(shape, 1 - out_dim)
        return (
            (into // SUB == out // plan.rest) & (into % SUB == cut * plan.rest + out % plan.rest)
        ).astype(jnp.bfloat16)

    def unpack(which, b):
        at = pl.ds(pl.multiple_of(b * lead * SUB, SUB), lead * SUB)
        for f in range(plan.full):
            rows_ref[f * lead * SUB : (f + 1) * lead * SUB, :] = recv_ref[
                which, at, f * width : (f + 1) * width
            ]
        for c in range(plan.cuts):
            pick = rest_pick(c, (rest_rows, lead * SUB), 0)
            rows_ref[full_rows:, c * plan.cut : (c + 1) * plan.cut] = dot(
                pick, recv_ref[which, at, plan.full * width :]
            ).astype(jnp.bfloat16)

    def repack(b):
        at = pl.ds(pl.multiple_of(b * lead * SUB, SUB), lead * SUB)
        for f in range(plan.full):
            part_ref[at, f * width : (f + 1) * width] = rows_ref[f * lead * SUB : (f + 1) * lead * SUB, :]
        if plan.rest:
            total = None
            for c in range(plan.cuts):
                pick = rest_pick(c, (lead * SUB, rest_rows), 1)
                part = dot(pick, rows_ref[full_rows:, c * plan.cut : (c + 1) * plan.cut])
                total = part if total is None else total + part
            part_ref[at, plan.full * width :] = total.astype(jnp.bfloat16)

    tile = 256

    def cols(i):
        return pl.ds(pl.multiple_of(i * tile, tile), tile)

    def hidden_block(b, carry):
        unpack(1, b)
        at = pl.ds(pl.multiple_of(b * block, SUB), block)

        def step(i, inner):
            hidden_ref[at, cols(i)] = dot(rows_ref[...], down_ref[cols(i), :], ((1,), (1,)))
            return inner

        return lax.fori_loop(0, hidden_width // tile, step, carry)

    def expert_block(b, carry):
        unpack(0, b)
        at = pl.ds(pl.multiple_of(b * block, SUB), block)

        def project(i, inner):
            gate_proj = dot(rows_ref[...], gate_ref[:, cols(i)])
            up_proj = dot(rows_ref[...], up_ref[:, cols(i)])
            hidden_grad = hidden_ref[at, cols(i)]
            sig = jax.nn.sigmoid(gate_proj)
            scaled = hidden_grad * sig
            both_ref[0, :, cols(i)] = (scaled * up_proj * (1.0 + gate_proj * (1.0 - sig))).astype(jnp.bfloat16)
            both_ref[1, :, cols(i)] = (scaled * gate_proj).astype(jnp.bfloat16)
            return inner

        lax.fori_loop(0, hidden_width // tile, project, 0)

        def collect(i, inner):
            total = dot(both_ref[0], gate_ref[cols(i), :], ((1,), (1,)))
            total = total + dot(both_ref[1], up_ref[cols(i), :], ((1,), (1,)))
            rows_ref[:, cols(i)] = total.astype(jnp.bfloat16)
            return inner

        lax.fori_loop(0, width // tile, collect, 0)
        repack(b)
        return carry

    pass_on(1)
    forwarded(1)
    weights[0].wait()
    lax.fori_loop(0, plan.blocks, hidden_block, 0)
    pass_on(0)
    weights[1].wait()
    weights[2].wait()
    forwarded(0)
    lax.fori_loop(0, plan.blocks, expert_block, 0)

    @pl.when(seq < last)
    def _():
        for c in halo(True):
            c.wait_send()

    @pl.when(seq > 0)
    def _():
        for c in halo(False):
            c.wait_send()

    finish(1)
    finish(0)


def backward_kernel(
    plan, ids_ref, gates_ref, part_ref, q_ref, grad_ref, gain_ref, prob_ref, unit_ref, inv_ref, vx_ref,
    key_ref, value_ref,
    rbuf, ssum, back, ag_ref, mid_ref, side_ref, side_in,
    send_sem, recv_sem, fsend, frecv, side_send, side_recv,
):
    seq, exp = place()
    local_len, width, rows = plan.local_len, plan.width, plan.rows
    member = seq % plan.group
    mine = seq // plan.group * plan.col_count + exp
    last = plan.seq_count - 1
    greet(plan)
    span = plan.dests // plan.pieces * SUB

    def summing(piece, other):
        to_member = (member + other) % plan.group
        return remote(
            part_ref.at[pl.ds(pl.multiple_of(to_member * rows + piece * span, SUB), span)],
            rbuf.at[other, pl.ds(piece * span, span)],
            fsend.at[piece, other],
            frecv.at[piece, other],
            (seq // plan.group * plan.group + to_member, exp),
        )

    for piece in range(plan.pieces):
        for other in range(1, plan.group):
            summing(piece, other).start()

    def chunk(dest):
        return pl.ds(pl.multiple_of(dest * SUB, SUB), SUB)

    def sending(dest):
        return remote(
            ssum.at[chunk(dest)], back.at[chunk(mine)], send_sem.at[dest], recv_sem.at[mine],
            partner(plan, dest, member),
        )

    def arriving(source):
        return remote(
            ssum.at[chunk(source)], back.at[chunk(source)], send_sem.at[source], recv_sem.at[source],
            partner(plan, source, member),
        )

    for piece in range(plan.pieces):
        for other in range(1, plan.group):
            summing(piece, other).wait_recv()
        at = pl.ds(piece * span, span)
        total = part_ref[pl.ds(pl.multiple_of(member * rows + piece * span, SUB), span), :].astype(jnp.float32)
        for other in range(1, plan.group):
            total = total + rbuf[other, at, :].astype(jnp.float32)
        ssum[at, :] = total.astype(jnp.bfloat16)

        def step(j, carry):
            dest = piece * (span // SUB) + j

            @pl.when(dest != mine)
            def _():
                sending(dest).start()

            return carry

        lax.fori_loop(0, span // SUB, step, 0)
    back[chunk(mine), :] = ssum[chunk(mine), :]

    blank = jnp.zeros((2, local_len, width), jnp.bfloat16)

    @pl.when(seq == 0)
    def _():
        side_in[0] = blank

    @pl.when(seq == last)
    def _():
        side_in[1] = blank

    expert = expert_of(plan, iota((local_len, plan.dests), 1))
    named = [ids_ref[:, j : j + 1] == expert for j in range(2)]
    routed = (named[0] | named[1]).astype(jnp.bfloat16)
    before = (iota((local_len, local_len), 1) < iota((local_len, local_len), 0)).astype(jnp.bfloat16)
    rank = dot(before, routed)
    spread = (iota((plan.dests, rows), 1) // SUB == iota((plan.dests, rows), 0)).astype(jnp.bfloat16)
    row = iota((local_len, rows), 1) % SUB
    slots = [
        dot(jnp.where(named[j], rank, -1.0).astype(jnp.bfloat16), spread).astype(jnp.int32) for j in range(2)
    ]

    def wait_back(j, carry):
        arriving((mine + j) % plan.dests).wait_recv()
        return carry

    lax.fori_loop(1, plan.dests, wait_back, 0)

    pieces = []
    blocks = plan.cuts if plan.rest else 1
    step_width = width // blocks
    for c in range(blocks):
        total = None
        for j in range(2):
            got = None
            for f in range(plan.full):
                pick = (slots[j] == row + f * SUB).astype(jnp.bfloat16)
                part = dot(pick, back[:, f * width + c * step_width : f * width + (c + 1) * step_width])
                got = part if got is None else got + part
            if plan.rest:
                pick = (slots[j] == row % plan.rest + plan.full * SUB) & (row // plan.rest == c)
                part = dot(pick.astype(jnp.bfloat16), back[:, plan.full * width :])
                got = part if got is None else got + part
            got = gates_ref[:, j : j + 1] * got
            total = got if total is None else total + got
        pieces.append(total)
    normed_grad = jnp.concatenate(pieces, axis=1)
    scaled = normed_grad * gain_ref[...]
    unit = unit_ref[...]
    inner = jnp.mean(scaled * unit, axis=-1, keepdims=True)
    attn_grad = grad_ref[...].astype(jnp.float32) + inv_ref[:, 0:1] * (scaled - unit * inner)
    ag_ref[...] = attn_grad.astype(jnp.bfloat16)

    parts = 4
    per = plan.heads // parts

    def side_copy(p, right):
        cols = pl.ds(p * per * HEAD_DIM, per * HEAD_DIM)
        d = 1 if right else 0
        to = (seq + 1, exp) if right else (seq - 1, exp)
        return remote(
            side_ref.at[d, :, :, cols], side_in.at[1 - d, :, :, cols],
            side_send.at[d, p], side_recv.at[1 - d, p], to,
        )

    for p in range(parts):
        for u in range(per):
            h = p * per + u
            at = slice(h * HEAD_DIM, (h + 1) * HEAD_DIM)
            vh = vx_ref[:, :, at].reshape(3 * local_len, HEAD_DIM)
            weights = prob_ref[h]
            grad_h = ag_ref[:, at]
            prob_grad = dot(vh, grad_h, ((1,), (1,)))
            inner_sum = jnp.sum(weights * prob_grad, axis=0, keepdims=True)
            score_grad = (weights * (prob_grad - inner_sum)).astype(jnp.bfloat16)
            key_part = dot(score_grad, q_ref[:, at]) * HEAD_DIM ** (-0.5)
            value_part = dot(weights.astype(jnp.bfloat16), grad_h)
            for i, part in enumerate((key_part, value_part)):
                side_ref[0, i, :, at] = part[:local_len].astype(jnp.bfloat16)
                mid_ref[i, :, at] = part[local_len : 2 * local_len]
                side_ref[1, i, :, at] = part[2 * local_len :].astype(jnp.bfloat16)

        @pl.when(seq > 0)
        def _():
            side_copy(p, False).start()

        @pl.when(seq < last)
        def _():
            side_copy(p, True).start()

    for p in range(parts):
        @pl.when(seq > 0)
        def _():
            side_copy(p, True).wait_recv()

        @pl.when(seq < last)
        def _():
            side_copy(p, False).wait_recv()

        at = slice(p * per * HEAD_DIM, (p + 1) * per * HEAD_DIM)
        for i, ref in enumerate((key_ref, value_ref)):
            total = mid_ref[i, :, at] + side_in[0, i, :, at].astype(jnp.float32)
            ref[:, at] = (total + side_in[1, i, :, at].astype(jnp.float32)).astype(jnp.bfloat16)

    for p in range(parts):
        @pl.when(seq > 0)
        def _():
            side_copy(p, False).wait_send()

        @pl.when(seq < last)
        def _():
            side_copy(p, True).wait_send()

    for piece in range(plan.pieces):
        for other in range(1, plan.group):
            summing(piece, other).wait_send()

    def wait_sent(j, carry):
        sending((mine + j) % plan.dests).wait_send()
        return carry

    lax.fori_loop(1, plan.dests, wait_sent, 0)


def on_device(
    queries,
    keys,
    values,
    out_grad,
    norm_gain,
    gate_values,
    expert_ids,
    tile_offsets,
    gate_weight,
    up_weight,
    down_weight,
):
    local_len, width = queries.shape[1:]
    plan = Plan(local_len, width, lax.axis_size("seq"), lax.axis_size("exp"))
    gain = norm_gain.reshape(1, width)
    group, rows, packed = plan.group, plan.rows, plan.packed
    vmem = pl.BlockSpec(memory_space=pltpu.VMEM)
    smem = pl.BlockSpec(memory_space=pltpu.SMEM)
    bf16, f32 = jnp.bfloat16, jnp.float32
    hidden = gate_weight.shape[3]
    dma = pltpu.SemaphoreType.DMA
    partial_value, prob, unit, inv, vx = pl.pallas_call(
        functools.partial(forward_kernel, plan),
        out_shape=(
            jax.ShapeDtypeStruct((group * rows, packed), bf16),
            jax.ShapeDtypeStruct((plan.heads, 3 * local_len, local_len), f32),
            jax.ShapeDtypeStruct((local_len, width), f32),
            jax.ShapeDtypeStruct((local_len, 128), f32),
            jax.ShapeDtypeStruct((3, local_len, width), bf16),
        ),
        in_specs=[smem] + [vmem] * 6 + [pl.BlockSpec(memory_space=pl.ANY)] * 3,
        out_specs=(vmem,) * 5,
        scratch_shapes=[
            pltpu.VMEM((2, group * rows, packed), bf16),
            pltpu.VMEM((3, local_len, width), bf16),
            pltpu.VMEM((local_len, width), bf16),
            pltpu.VMEM((2, rows, packed), bf16),
            pltpu.VMEM((local_len, width), f32),
            pltpu.VMEM((width, hidden), bf16),
            pltpu.VMEM((width, hidden), bf16),
            pltpu.VMEM((hidden, width), bf16),
            pltpu.VMEM((plan.block_rows, width), bf16),
            pltpu.VMEM((plan.blocks * plan.block_rows, hidden), f32),
            pltpu.VMEM((2, plan.block_rows, hidden), bf16),
            dma((3,)),
            dma((2, 2)),
            dma((2, 2)),
            dma((2, plan.dests)),
            dma((2, plan.dests)),
            dma((2, plan.pieces, group)),
            dma((2, plan.pieces, group)),
        ],
        compiler_params=pltpu.CompilerParams(
            collective_id=0, has_side_effects=True, vmem_limit_bytes=60 * 2**20
        ),
        name="attend_and_dispatch",
    )(
        tile_offsets[0], expert_ids[0].T, queries[0], keys[0], values[0], out_grad[0], gain,
        gate_weight[0, 0], up_weight[0, 0], down_weight[0, 0],
    )
    key_out, value_out = pl.pallas_call(
        functools.partial(backward_kernel, plan),
        out_shape=(jax.ShapeDtypeStruct((local_len, width), bf16),) * 2,
        in_specs=[vmem] * 10,
        out_specs=(vmem,) * 2,
        scratch_shapes=[
            pltpu.VMEM((group, rows, packed), bf16),
            pltpu.VMEM((rows, packed), bf16),
            pltpu.VMEM((rows, packed), bf16),
            pltpu.VMEM((local_len, width), bf16),
            pltpu.VMEM((2, local_len, width), f32),
            pltpu.VMEM((2, 2, local_len, width), bf16),
            pltpu.VMEM((2, 2, local_len, width), bf16),
            dma((plan.dests,)),
            dma((plan.dests,)),
            dma((plan.pieces, group)),
            dma((plan.pieces, group)),
            dma((2, 4)),
            dma((2, 4)),
        ],
        compiler_params=pltpu.CompilerParams(
            collective_id=1, has_side_effects=True, vmem_limit_bytes=60 * 2**20
        ),
        name="combine_and_attend_back",
    )(expert_ids[0], gate_values[0], partial_value, queries[0], out_grad[0], gain, prob, unit, inv, vx)
    return (key_out[None], value_out[None])


def solution(mesh):
    return jax.shard_map(
        on_device,
        mesh=mesh,
        in_specs=(
            P("exp", "seq", None),
            P("exp", "seq", None),
            P("exp", "seq", None),
            P("exp", "seq", None),
            P(),
            P("exp", "seq", None),
            P("exp", "seq", None),
            P("exp", "seq", None),
            P("exp", "seq", None, None),
            P("exp", "seq", None, None),
            P("exp", "seq", None, None),
        ),
        out_specs=(P("exp", "seq", None), P("exp", "seq", None)),
        check_vma=False,
    )
```

```python
import functools

import jax
import jax.numpy as jnp
from jax import lax
from jax.experimental import pallas as pl
from jax.experimental.pallas import tpu as pltpu
from jax.sharding import PartitionSpec as P

HEAD_DIM = 128
TILE = 64
SUB = 16
MESH = pl.DeviceIdType.MESH

epsilon = 1e-06


def dot(a, b, dims=((1,), (0,))):
    return lax.dot_general(a, b, (dims, ((), ())), preferred_element_type=jnp.float32)


def iota(shape, dim):
    return lax.broadcasted_iota(jnp.int32, shape, dim)


class Plan:
    def __init__(self, local_len, width, seq_count, col_count):
        self.local_len, self.width = local_len, width
        self.seq_count, self.col_count = seq_count, col_count
        self.group = seq_count // 2
        self.heads = width // HEAD_DIM
        experts = 2 * col_count
        capacity = max(2, (5 * local_len + 2 * experts - 1) // (2 * experts))
        self.full = capacity // SUB
        left = capacity % SUB
        self.rest = 0 if left == 0 else 4 if left <= 4 else 8 if left <= 8 else 16
        if self.rest == 16:
            self.full, self.rest = self.full + 1, 0
        self.cuts = SUB // self.rest if self.rest else 0
        self.cut = width // self.cuts if self.rest else 0
        self.packed = self.full * width + self.cut
        self.dests = 2 * col_count
        self.rows = self.dests * SUB
        self.pieces = 4
        self.lead = min(32, self.group * self.dests)
        self.blocks = self.group * self.dests // self.lead
        self.block_rows = self.lead * (self.full * SUB + self.rest)


def expert_of(plan, dest):
    return 2 * (dest % plan.col_count) + dest // plan.col_count


def partner(plan, dest, member):
    return (dest // plan.col_count * plan.group + member, dest % plan.col_count)


def place():
    return lax.axis_index("seq"), lax.axis_index("exp")


def crosses(plan, seq, side):
    other = seq + side
    return (other >= 0) & (other < plan.seq_count) & (other // plan.group != seq // plan.group)


def greet(plan):
    seq, exp = place()
    member = seq % plan.group
    mine = seq // plan.group * plan.col_count + exp
    barrier = pltpu.get_barrier_semaphore()

    def step(j, carry):
        dest = (mine + j) % plan.dests
        pl.semaphore_signal(barrier, inc=1, device_id=partner(plan, dest, member), device_id_type=MESH)
        return carry

    lax.fori_loop(1, plan.dests, step, 0)
    for other in range(1, plan.group):
        to = seq // plan.group * plan.group + (member + other) % plan.group
        pl.semaphore_signal(barrier, inc=1, device_id=(to, exp), device_id_type=MESH)
    low, high = crosses(plan, seq, -1), crosses(plan, seq, 1)

    @pl.when(low)
    def _():
        pl.semaphore_signal(barrier, inc=1, device_id=(seq - 1, exp), device_id_type=MESH)

    @pl.when(high)
    def _():
        pl.semaphore_signal(barrier, inc=1, device_id=(seq + 1, exp), device_id_type=MESH)

    peers = plan.dests - 1 + plan.group - 1
    pl.semaphore_wait(barrier, peers + jnp.where(low, 1, 0) + jnp.where(high, 1, 0))


def remote(src, dst, send, recv, to):
    return pltpu.make_async_remote_copy(
        src_ref=src, dst_ref=dst, send_sem=send, recv_sem=recv, device_id=to, device_id_type=MESH
    )


def window_mask(plan, offs_ref, seq):
    tiles = plan.local_len // TILE
    key_tile = iota((3 * plan.local_len, plan.local_len), 0) // TILE
    query_tile = iota((3 * plan.local_len, plan.local_len), 1) // TILE
    mask = jnp.zeros((3 * plan.local_len, plan.local_len), jnp.int32)
    for i in range(tiles):
        for m in range(offs_ref.shape[1]):
            offset = offs_ref[i, m]
            whole = seq * tiles + i + offset
            inside = (whole >= 0) & (whole < tiles * plan.seq_count)
            target = jnp.where(inside, tiles + i + offset, -1)
            mask = mask | ((query_tile == i) & (key_tile == target)).astype(jnp.int32)
    return mask > 0


def forward_kernel(
    plan, offs_ref, ids_ref, q_ref, k_ref, v_ref, grad_ref, gain_ref, gate_hbm, up_hbm, down_hbm,
    part_ref, prob_ref, unit_ref, inv_ref, vx_ref,
    recv_ref, kx_ref, normed_ref, sbuf, out_ref,
    gate_ref, up_ref, down_ref, rows_ref, hidden_ref, both_ref, weight_sem,
    halo_send, halo_recv, send_sem, recv_sem, fsend, frecv,
):
    seq, exp = place()
    local_len, width, rows = plan.local_len, plan.width, plan.rows
    member = seq % plan.group
    mine = seq // plan.group * plan.col_count + exp
    last = plan.seq_count - 1
    weights = [
        pltpu.make_async_copy(src, dst, weight_sem.at[i])
        for i, (src, dst) in enumerate(((down_hbm, down_ref), (gate_hbm, gate_ref), (up_hbm, up_ref)))
    ]
    for c in weights:
        c.start()
    greet(plan)

    def halo(right):
        to = (seq + 1, exp) if right else (seq - 1, exp)
        slot = 0 if right else 2
        d = 0 if right else 1
        return [
            remote(ref, ext.at[slot], halo_send.at[i, d], halo_recv.at[i, d], to)
            for i, (ref, ext) in enumerate(((k_ref, kx_ref), (v_ref, vx_ref)))
        ]

    @pl.when(seq < last)
    def _():
        for c in halo(True):
            c.start()

    @pl.when(seq > 0)
    def _():
        for c in halo(False):
            c.start()

    expert = expert_of(plan, iota((plan.dests, local_len), 0))
    routed = ((ids_ref[0:1, :] == expert) | (ids_ref[1:2, :] == expert)).astype(jnp.float32)
    before = (iota((local_len, local_len), 0) < iota((local_len, local_len), 1)).astype(jnp.bfloat16)
    rank = dot(routed.astype(jnp.bfloat16), before)
    held = jnp.where(routed > 0, rank, -1.0).astype(jnp.bfloat16)
    spread = (iota((rows, plan.dests), 0) // SUB == iota((rows, plan.dests), 1)).astype(jnp.bfloat16)
    slot_of = dot(spread, held).astype(jnp.int32)
    row = iota((rows, local_len), 0) % SUB

    def pack(which, rows_ref):
        for f in range(plan.full):
            pick = (slot_of == row + f * SUB).astype(jnp.bfloat16)
            sbuf[which, :, f * width : (f + 1) * width] = dot(pick, rows_ref[...]).astype(jnp.bfloat16)
        if plan.rest:
            total = None
            for c in range(plan.cuts):
                pick = (slot_of == row % plan.rest + plan.full * SUB) & (row // plan.rest == c)
                part = dot(pick.astype(jnp.bfloat16), rows_ref[:, c * plan.cut : (c + 1) * plan.cut])
                total = part if total is None else total + part
            sbuf[which, :, plan.full * width :] = total.astype(jnp.bfloat16)

    def chunk(dest):
        return pl.ds(pl.multiple_of(dest * SUB, SUB), SUB)

    def landed(dest):
        return pl.ds(pl.multiple_of((member * plan.dests + dest) * SUB, SUB), SUB)

    def sending(which, dest):
        return remote(
            sbuf.at[which, chunk(dest)],
            recv_ref.at[which, landed(mine)],
            send_sem.at[which, dest],
            recv_sem.at[which, mine],
            partner(plan, dest, member),
        )

    def arriving(which, source):
        return remote(
            sbuf.at[which, chunk(source)],
            recv_ref.at[which, landed(source)],
            send_sem.at[which, source],
            recv_sem.at[which, source],
            partner(plan, source, member),
        )

    def send_all(which):
        def step(j, carry):
            sending(which, (mine + j) % plan.dests).start()
            return carry

        lax.fori_loop(1, plan.dests, step, 0)
        recv_ref[which, landed(mine), :] = sbuf[which, chunk(mine), :]

    span = plan.dests // plan.pieces

    def passing(which, piece, other, owner):
        at = pl.ds(pl.multiple_of((owner * plan.dests + piece * span) * SUB, SUB), span * SUB)
        to = (seq // plan.group * plan.group + (member + other) % plan.group, exp)
        return remote(
            recv_ref.at[which, at],
            recv_ref.at[which, at],
            fsend.at[which, piece, other],
            frecv.at[which, piece, owner],
            to,
        )

    def pass_on(which):
        for k in range(plan.pieces):
            piece = (mine // span + plan.pieces - k) % plan.pieces

            def step(j, carry):
                source = piece * span + j

                @pl.when(source != mine)
                def _():
                    arriving(which, source).wait_recv()

                return carry

            lax.fori_loop(0, span, step, 0)
            for other in range(1, plan.group):
                passing(which, piece, other, member).start()

    def forwarded(which):
        for piece in range(plan.pieces):
            for other in range(1, plan.group):
                owner = (member + plan.group - other) % plan.group
                passing(which, piece, other, owner).wait_recv()

    def finish(which):
        for piece in range(plan.pieces):
            for other in range(1, plan.group):
                passing(which, piece, other, member).wait_send()

        def step(j, carry):
            sending(which, (mine + j) % plan.dests).wait_send()
            return carry

        lax.fori_loop(1, plan.dests, step, 0)

    pack(1, grad_ref)
    send_all(1)

    kx_ref[1] = k_ref[...]
    vx_ref[1] = v_ref[...]
    blank = jnp.zeros((local_len, width), jnp.bfloat16)

    @pl.when(seq == 0)
    def _():
        kx_ref[0] = blank
        vx_ref[0] = blank

    @pl.when(seq == last)
    def _():
        kx_ref[2] = blank
        vx_ref[2] = blank

    mask = window_mask(plan, offs_ref, seq)

    @pl.when(seq > 0)
    def _():
        for c in halo(True):
            c.wait_recv()

    @pl.when(seq < last)
    def _():
        for c in halo(False):
            c.wait_recv()

    per = 4

    def heads(i, carry):
        for u in range(per):
            h = i * per + u
            at = pl.ds(pl.multiple_of(h * HEAD_DIM, HEAD_DIM), HEAD_DIM)
            kh = kx_ref[:, :, at].reshape(3 * local_len, HEAD_DIM)
            vh = vx_ref[:, :, at].reshape(3 * local_len, HEAD_DIM)
            scores = dot(kh, q_ref[:, at], ((1,), (1,))) * HEAD_DIM ** (-0.5)
            scores = jnp.where(mask, scores, -jnp.inf)
            raised = jnp.exp(scores - jnp.max(scores, axis=0, keepdims=True))
            weights = raised / jnp.sum(raised, axis=0, keepdims=True)
            prob_ref[h] = weights
            out_ref[:, at] = dot(weights.astype(jnp.bfloat16), vh, ((0,), (0,)))
        return carry

    lax.fori_loop(0, plan.heads // per, heads, 0)

    attn_out = out_ref[...]
    inv_rms = lax.rsqrt(jnp.mean(attn_out * attn_out, axis=-1, keepdims=True) + epsilon)
    unit = attn_out * inv_rms
    unit_ref[...] = unit
    inv_ref[...] = jnp.broadcast_to(inv_rms, (local_len, 128))
    normed_ref[...] = (unit * gain_ref[...]).astype(jnp.bfloat16)
    pack(0, normed_ref)
    send_all(0)
    lead, full_rows = plan.lead, plan.lead * plan.full * SUB
    rest_rows, block = plan.lead * plan.rest, plan.block_rows
    hidden_width = gate_ref.shape[1]

    def rest_pick(cut, shape, out_dim):
        out, into = iota(shape, out_dim), iota(shape, 1 - out_dim)
        return (
            (into // SUB == out // plan.rest) & (into % SUB == cut * plan.rest + out % plan.rest)
        ).astype(jnp.bfloat16)

    def unpack(which, b):
        at = pl.ds(pl.multiple_of(b * lead * SUB, SUB), lead * SUB)
        for f in range(plan.full):
            rows_ref[f * lead * SUB : (f + 1) * lead * SUB, :] = recv_ref[
                which, at, f * width : (f + 1) * width
            ]
        for c in range(plan.cuts):
            pick = rest_pick(c, (rest_rows, lead * SUB), 0)
            rows_ref[full_rows:, c * plan.cut : (c + 1) * plan.cut] = dot(
                pick, recv_ref[which, at, plan.full * width :]
            ).astype(jnp.bfloat16)

    def repack(b):
        at = pl.ds(pl.multiple_of(b * lead * SUB, SUB), lead * SUB)
        for f in range(plan.full):
            part_ref[at, f * width : (f + 1) * width] = rows_ref[f * lead * SUB : (f + 1) * lead * SUB, :]
        if plan.rest:
            total = None
            for c in range(plan.cuts):
                pick = rest_pick(c, (lead * SUB, rest_rows), 1)
                part = dot(pick, rows_ref[full_rows:, c * plan.cut : (c + 1) * plan.cut])
                total = part if total is None else total + part
            part_ref[at, plan.full * width :] = total.astype(jnp.bfloat16)

    tile = 256

    def cols(i):
        return pl.ds(pl.multiple_of(i * tile, tile), tile)

    def hidden_block(b, carry):
        unpack(1, b)
        at = pl.ds(pl.multiple_of(b * block, SUB), block)

        def step(i, inner):
            hidden_ref[at, cols(i)] = dot(rows_ref[...], down_ref[cols(i), :], ((1,), (1,)))
            return inner

        return lax.fori_loop(0, hidden_width // tile, step, carry)

    def expert_block(b, carry):
        unpack(0, b)
        at = pl.ds(pl.multiple_of(b * block, SUB), block)

        def project(i, inner):
            gate_proj = dot(rows_ref[...], gate_ref[:, cols(i)])
            up_proj = dot(rows_ref[...], up_ref[:, cols(i)])
            hidden_grad = hidden_ref[at, cols(i)]
            sig = jax.nn.sigmoid(gate_proj)
            scaled = hidden_grad * sig
            both_ref[0, :, cols(i)] = (scaled * up_proj * (1.0 + gate_proj * (1.0 - sig))).astype(jnp.bfloat16)
            both_ref[1, :, cols(i)] = (scaled * gate_proj).astype(jnp.bfloat16)
            return inner

        lax.fori_loop(0, hidden_width // tile, project, 0)

        def collect(i, inner):
            total = dot(both_ref[0], gate_ref[cols(i), :], ((1,), (1,)))
            total = total + dot(both_ref[1], up_ref[cols(i), :], ((1,), (1,)))
            rows_ref[:, cols(i)] = total.astype(jnp.bfloat16)
            return inner

        lax.fori_loop(0, width // tile, collect, 0)
        repack(b)
        return carry

    pass_on(1)
    forwarded(1)
    weights[0].wait()
    lax.fori_loop(0, plan.blocks, hidden_block, 0)
    pass_on(0)
    weights[1].wait()
    weights[2].wait()
    forwarded(0)
    lax.fori_loop(0, plan.blocks, expert_block, 0)

    @pl.when(seq < last)
    def _():
        for c in halo(True):
            c.wait_send()

    @pl.when(seq > 0)
    def _():
        for c in halo(False):
            c.wait_send()

    finish(1)
    finish(0)


def backward_kernel(
    plan, ids_ref, gates_ref, part_ref, q_ref, grad_ref, gain_ref, prob_ref, unit_ref, inv_ref, vx_ref,
    key_ref, value_ref,
    rbuf, ssum, back, ag_ref, mid_ref, side_ref, side_in,
    send_sem, recv_sem, fsend, frecv, side_send, side_recv,
):
    seq, exp = place()
    local_len, width, rows = plan.local_len, plan.width, plan.rows
    member = seq % plan.group
    mine = seq // plan.group * plan.col_count + exp
    last = plan.seq_count - 1
    greet(plan)
    span = plan.dests // plan.pieces * SUB

    def summing(piece, other):
        to_member = (member + other) % plan.group
        return remote(
            part_ref.at[pl.ds(pl.multiple_of(to_member * rows + piece * span, SUB), span)],
            rbuf.at[other, pl.ds(pl.multiple_of(piece * span, SUB), span)],
            fsend.at[piece, other],
            frecv.at[piece, other],
            (seq // plan.group * plan.group + to_member, exp),
        )

    chunks = span // SUB

    def turn(k):
        return (mine // chunks + k) % plan.pieces

    for k in range(plan.pieces):
        for other in range(1, plan.group):
            summing(turn(k), other).start()

    def chunk(dest):
        return pl.ds(pl.multiple_of(dest * SUB, SUB), SUB)

    def sending(dest):
        return remote(
            ssum.at[chunk(dest)], back.at[chunk(mine)], send_sem.at[dest], recv_sem.at[mine],
            partner(plan, dest, member),
        )

    def arriving(source):
        return remote(
            ssum.at[chunk(source)], back.at[chunk(source)], send_sem.at[source], recv_sem.at[source],
            partner(plan, source, member),
        )

    for k in range(plan.pieces):
        piece = turn(k)
        for other in range(1, plan.group):
            summing(piece, other).wait_recv()
        at = pl.ds(pl.multiple_of(piece * span, SUB), span)
        total = part_ref[pl.ds(pl.multiple_of(member * rows + piece * span, SUB), span), :].astype(jnp.float32)
        for other in range(1, plan.group):
            total = total + rbuf[other, at, :].astype(jnp.float32)
        ssum[at, :] = total.astype(jnp.bfloat16)

        def step(j, carry, piece=piece):
            dest = piece * chunks + (mine + j) % chunks

            @pl.when(dest != mine)
            def _():
                sending(dest).start()

            return carry

        lax.fori_loop(0, chunks, step, 0)
    back[chunk(mine), :] = ssum[chunk(mine), :]

    blank = jnp.zeros((2, local_len, width), jnp.bfloat16)

    @pl.when(seq == 0)
    def _():
        side_in[0] = blank

    @pl.when(seq == last)
    def _():
        side_in[1] = blank

    expert = expert_of(plan, iota((local_len, plan.dests), 1))
    named = [ids_ref[:, j : j + 1] == expert for j in range(2)]
    routed = (named[0] | named[1]).astype(jnp.bfloat16)
    before = (iota((local_len, local_len), 1) < iota((local_len, local_len), 0)).astype(jnp.bfloat16)
    rank = dot(before, routed)
    spread = (iota((plan.dests, rows), 1) // SUB == iota((plan.dests, rows), 0)).astype(jnp.bfloat16)
    row = iota((local_len, rows), 1) % SUB
    slots = [
        dot(jnp.where(named[j], rank, -1.0).astype(jnp.bfloat16), spread).astype(jnp.int32) for j in range(2)
    ]

    def wait_back(j, carry):
        arriving((mine + j) % plan.dests).wait_recv()
        return carry

    lax.fori_loop(1, plan.dests, wait_back, 0)

    pieces = []
    blocks = plan.cuts if plan.rest else 1
    step_width = width // blocks
    for c in range(blocks):
        total = None
        for j in range(2):
            got = None
            for f in range(plan.full):
                pick = (slots[j] == row + f * SUB).astype(jnp.bfloat16)
                part = dot(pick, back[:, f * width + c * step_width : f * width + (c + 1) * step_width])
                got = part if got is None else got + part
            if plan.rest:
                pick = (slots[j] == row % plan.rest + plan.full * SUB) & (row // plan.rest == c)
                part = dot(pick.astype(jnp.bfloat16), back[:, plan.full * width :])
                got = part if got is None else got + part
            got = gates_ref[:, j : j + 1] * got
            total = got if total is None else total + got
        pieces.append(total)
    normed_grad = jnp.concatenate(pieces, axis=1)
    scaled = normed_grad * gain_ref[...]
    unit = unit_ref[...]
    inner = jnp.mean(scaled * unit, axis=-1, keepdims=True)
    attn_grad = grad_ref[...].astype(jnp.float32) + inv_ref[:, 0:1] * (scaled - unit * inner)
    ag_ref[...] = attn_grad.astype(jnp.bfloat16)

    parts = 4
    per = plan.heads // parts

    def side_copy(p, right):
        cols = pl.ds(p * per * HEAD_DIM, per * HEAD_DIM)
        d = 1 if right else 0
        to = (seq + 1, exp) if right else (seq - 1, exp)
        return remote(
            side_ref.at[d, :, :, cols], side_in.at[1 - d, :, :, cols],
            side_send.at[d, p], side_recv.at[1 - d, p], to,
        )

    for p in range(parts):
        for u in range(per):
            h = p * per + u
            at = slice(h * HEAD_DIM, (h + 1) * HEAD_DIM)
            vh = vx_ref[:, :, at].reshape(3 * local_len, HEAD_DIM)
            weights = prob_ref[h]
            grad_h = ag_ref[:, at]
            prob_grad = dot(vh, grad_h, ((1,), (1,)))
            inner_sum = jnp.sum(weights * prob_grad, axis=0, keepdims=True)
            score_grad = (weights * (prob_grad - inner_sum)).astype(jnp.bfloat16)
            key_part = dot(score_grad, q_ref[:, at]) * HEAD_DIM ** (-0.5)
            value_part = dot(weights.astype(jnp.bfloat16), grad_h)
            for i, part in enumerate((key_part, value_part)):
                side_ref[0, i, :, at] = part[:local_len].astype(jnp.bfloat16)
                mid_ref[i, :, at] = part[local_len : 2 * local_len]
                side_ref[1, i, :, at] = part[2 * local_len :].astype(jnp.bfloat16)

        @pl.when(seq > 0)
        def _():
            side_copy(p, False).start()

        @pl.when(seq < last)
        def _():
            side_copy(p, True).start()

    for p in range(parts):
        @pl.when(seq > 0)
        def _():
            side_copy(p, True).wait_recv()

        @pl.when(seq < last)
        def _():
            side_copy(p, False).wait_recv()

        at = slice(p * per * HEAD_DIM, (p + 1) * per * HEAD_DIM)
        for i, ref in enumerate((key_ref, value_ref)):
            total = mid_ref[i, :, at] + side_in[0, i, :, at].astype(jnp.float32)
            ref[:, at] = (total + side_in[1, i, :, at].astype(jnp.float32)).astype(jnp.bfloat16)

    for p in range(parts):
        @pl.when(seq > 0)
        def _():
            side_copy(p, False).wait_send()

        @pl.when(seq < last)
        def _():
            side_copy(p, True).wait_send()

    for piece in range(plan.pieces):
        for other in range(1, plan.group):
            summing(piece, other).wait_send()

    def wait_sent(j, carry):
        sending((mine + j) % plan.dests).wait_send()
        return carry

    lax.fori_loop(1, plan.dests, wait_sent, 0)


def on_device(
    queries,
    keys,
    values,
    out_grad,
    norm_gain,
    gate_values,
    expert_ids,
    tile_offsets,
    gate_weight,
    up_weight,
    down_weight,
):
    local_len, width = queries.shape[1:]
    plan = Plan(local_len, width, lax.axis_size("seq"), lax.axis_size("exp"))
    gain = norm_gain.reshape(1, width)
    group, rows, packed = plan.group, plan.rows, plan.packed
    vmem = pl.BlockSpec(memory_space=pltpu.VMEM)
    smem = pl.BlockSpec(memory_space=pltpu.SMEM)
    bf16, f32 = jnp.bfloat16, jnp.float32
    hidden = gate_weight.shape[3]
    dma = pltpu.SemaphoreType.DMA
    partial_value, prob, unit, inv, vx = pl.pallas_call(
        functools.partial(forward_kernel, plan),
        out_shape=(
            jax.ShapeDtypeStruct((group * rows, packed), bf16),
            jax.ShapeDtypeStruct((plan.heads, 3 * local_len, local_len), f32),
            jax.ShapeDtypeStruct((local_len, width), f32),
            jax.ShapeDtypeStruct((local_len, 128), f32),
            jax.ShapeDtypeStruct((3, local_len, width), bf16),
        ),
        in_specs=[smem] + [vmem] * 6 + [pl.BlockSpec(memory_space=pl.ANY)] * 3,
        out_specs=(vmem,) * 5,
        scratch_shapes=[
            pltpu.VMEM((2, group * rows, packed), bf16),
            pltpu.VMEM((3, local_len, width), bf16),
            pltpu.VMEM((local_len, width), bf16),
            pltpu.VMEM((2, rows, packed), bf16),
            pltpu.VMEM((local_len, width), f32),
            pltpu.VMEM((width, hidden), bf16),
            pltpu.VMEM((width, hidden), bf16),
            pltpu.VMEM((hidden, width), bf16),
            pltpu.VMEM((plan.block_rows, width), bf16),
            pltpu.VMEM((plan.blocks * plan.block_rows, hidden), f32),
            pltpu.VMEM((2, plan.block_rows, hidden), bf16),
            dma((3,)),
            dma((2, 2)),
            dma((2, 2)),
            dma((2, plan.dests)),
            dma((2, plan.dests)),
            dma((2, plan.pieces, group)),
            dma((2, plan.pieces, group)),
        ],
        compiler_params=pltpu.CompilerParams(
            collective_id=0, has_side_effects=True, vmem_limit_bytes=60 * 2**20
        ),
        name="attend_and_dispatch",
    )(
        tile_offsets[0], expert_ids[0].T, queries[0], keys[0], values[0], out_grad[0], gain,
        gate_weight[0, 0], up_weight[0, 0], down_weight[0, 0],
    )
    key_out, value_out = pl.pallas_call(
        functools.partial(backward_kernel, plan),
        out_shape=(jax.ShapeDtypeStruct((local_len, width), bf16),) * 2,
        in_specs=[vmem] * 10,
        out_specs=(vmem,) * 2,
        scratch_shapes=[
            pltpu.VMEM((group, rows, packed), bf16),
            pltpu.VMEM((rows, packed), bf16),
            pltpu.VMEM((rows, packed), bf16),
            pltpu.VMEM((local_len, width), bf16),
            pltpu.VMEM((2, local_len, width), f32),
            pltpu.VMEM((2, 2, local_len, width), bf16),
            pltpu.VMEM((2, 2, local_len, width), bf16),
            dma((plan.dests,)),
            dma((plan.dests,)),
            dma((plan.pieces, group)),
            dma((plan.pieces, group)),
            dma((2, 4)),
            dma((2, 4)),
        ],
        compiler_params=pltpu.CompilerParams(
            collective_id=1, has_side_effects=True, vmem_limit_bytes=60 * 2**20
        ),
        name="combine_and_attend_back",
    )(expert_ids[0], gate_values[0], partial_value, queries[0], out_grad[0], gain, prob, unit, inv, vx)
    return (key_out[None], value_out[None])


def solution(mesh):
    return jax.shard_map(
        on_device,
        mesh=mesh,
        in_specs=(
            P("exp", "seq", None),
            P("exp", "seq", None),
            P("exp", "seq", None),
            P("exp", "seq", None),
            P(),
            P("exp", "seq", None),
            P("exp", "seq", None),
            P("exp", "seq", None),
            P("exp", "seq", None, None),
            P("exp", "seq", None, None),
            P("exp", "seq", None, None),
        ),
        out_specs=(P("exp", "seq", None), P("exp", "seq", None)),
        check_vma=False,
    )
```
